32 devices in a mesh: ga: 2 (over y), gx: 4 (over z), yz: 4 (over x, core).
Axes of the slice: x: 2, y: 2, z: 4, core: 2. Of those that a mesh axis runs over, the one named last changes fastest.
Arguments:
- tokens: bfloat16 [128, 18432], P(('ga', 'yz'), 'gx'), parts along dimension 0, may hold values from -6 to 6
- w_query: bfloat16 [18432, 12288], P('gx', 'yz'), may hold values from -0.046875 to 0.046875
- w_keyval: bfloat16 [18432, 512], P('gx', 'yz'), may hold values from -0.046875 to 0.046875
- w_out: bfloat16 [12288, 18432], P('yz', 'gx'), may hold values from -0.4375 to 0.4375
- cache_keys: bfloat16 [128, 512, 256], P(('ga', 'yz'), 'gx'), parts along dimension 0, may hold values from -720 to 720
- cache_values: bfloat16 [128, 512, 256], P(('ga', 'yz'), 'gx'), parts along dimension 0, may hold values from -6 to 6
- lengths: int32 [128], P(('ga', 'yz')), parts along dimension 0, may hold values from 128 to 512, as said below
- positions: int32 [128], P(('ga', 'yz')), parts along dimension 0, may hold values from 0 to 4095
Outputs:
- attended: bfloat16 [128, 18432], P(('ga', 'yz'), 'gx'), parts along dimension 0
The draws below stay inside these ranges and needn't reach their ends.
There are 2 independent parts, one for each index of `ga`. The reference program is written for one: setup_inputs(seed, part) draws one part's arguments, and reference() takes and returns one part's arrays. A program takes and returns all parts, laid end to end along the dimension named above; an argument that names none is the same for every part. Nothing has to cross between parts.
Inputs may be any that keep to these rules, and one draw needn't show every extreme that they name: `lengths`: some row holds all 512 slots and some row a quarter of them.
All inputs are finite; a program needn't handle non-finite values.
Results may differ from the reference program's by a relative error of at most 0.0055.
The reference program's roundings to bfloat16 on the way (of `query`, `keyval` and `out_heads`) count: a program that leaves them out, or rounds other values in their place, can miss the bound.
Values may be sent and summed in bfloat16 or wider, within the bound.
A program may use at most 128 MiB of HBM per device.

```python
import math
import jax
import jax.numpy as jnp
from jax import lax

D = 18432
HEADS = 48
HEAD_DIM = 256
CACHE = 512
HQ = 12288
ROWS = 64


def draw_cache_keys(key, part):
    key = jax.random.fold_in(key, 11)
    key_base = jax.random.fold_in(key, 0)
    base = jnp.clip(jax.random.normal(key_base, (ROWS, CACHE, HEAD_DIM), jnp.float32), -6.0, 6.0)
    return base.astype(jnp.bfloat16)


def draw_lengths(key, part):
    key = jax.random.fold_in(key, 5)
    key_len, key_full, key_step = jax.random.split(key, 3)
    filled = jax.random.randint(key_len, (ROWS,), CACHE // 4, CACHE + 1, jnp.int32)
    full_row = jax.random.randint(key_full, (), 0, ROWS, jnp.int32)
    short_row = (full_row + 1 + jax.random.randint(key_step, (), 0, ROWS - 1, jnp.int32)) % ROWS
    filled = filled.at[full_row].set(CACHE)
    filled = filled.at[short_row].set(CACHE // 4)
    return filled


def set_ends(entries, own_key, least, high):
    longest = entries.shape.index(max(entries.shape))
    spots = []
    for shift in (0, 1):
        where = [jax.random.randint(jax.random.fold_in(own_key, axis), (), 0, length) for axis, length in enumerate(entries.shape)]
        where[longest] = (where[longest] + shift) % entries.shape[longest]
        spots.append(tuple(where))
    return entries.at[spots[0]].set(least).at[spots[1]].set(high)


def levels(own_key, dims, cuts, smallest, largest):
    gain = 1.0
    for position, shards_of in cuts:
        heights = jax.random.uniform(jax.random.fold_in(jax.random.fold_in(own_key, 6), position), (shards_of,), jnp.float32, smallest / len(cuts), largest / len(cuts))
        gain = gain * jnp.repeat(jnp.exp(heights), dims[position] // shards_of).reshape((-1,) + (1,) * (len(dims) - 1 - position))
    return gain


def bell_draw(stream_key, shape, deviation, bound, pieces=(), held_as=jnp.bfloat16):
    result = jax.random.normal(stream_key, shape, jnp.float32) * deviation
    if len(pieces) > 0:
        result = levels(stream_key, shape, pieces, -0.22, 0.18) * result
    return jnp.clip(result, min=-bound, max=bound).astype(held_as)


def setup_inputs(seed: int = 0, part: int = 0) -> dict:
    splits = jax.random.split(jax.random.key(seed), 9)
    own_keys = jax.random.split(jax.random.fold_in(splits[8], part), 9)
    return {
        "tokens": bell_draw(own_keys[0], (ROWS, D), 1.0, 6.0, ((0, 4), (1, 4))),
        "w_query": bell_draw(splits[1], (D, HQ), D ** -0.5, 0.046875, ((0, 4), (1, 4))),
        "w_keyval": bell_draw(splits[2], (D, 2 * HEAD_DIM), D ** -0.5, 0.046875, ((0, 4), (1, 4))),
        "w_out": bell_draw(splits[3], (HQ, D), (HQ // 64) ** -0.5, 0.4375, ((0, 4), (1, 4))),
        "cache_keys": draw_cache_keys(jax.random.fold_in(jax.random.fold_in(splits[8], part), 71), part),
        "cache_values": bell_draw(own_keys[5], (ROWS, CACHE, HEAD_DIM), 1.0, 6.0, ((0, 4), (1, 4))),
        "lengths": draw_lengths(jax.random.fold_in(jax.random.fold_in(splits[8], part), 71), part),
        "positions": set_ends(jax.random.randint(own_keys[7], (ROWS,), 0, 4096), jax.random.fold_in(own_keys[7], 1), 0, 4095).astype(jnp.int32),
    }


def rotate(vectors, angles):
    half_dim = vectors.shape[-1] // 2
    first_half = vectors[..., :half_dim]
    second_half = vectors[..., half_dim:]
    cosines = jnp.cos(angles)
    sines = jnp.sin(angles)
    return jnp.concatenate([first_half * cosines - second_half * sines, first_half * sines + second_half * cosines], axis=-1)


def rotary_angles(positions, head_dim):
    half_dim = head_dim // 2
    inv_freq = jnp.exp(-jnp.arange(half_dim, dtype=jnp.float32) * (math.log(10000.0) / half_dim))
    return positions.astype(jnp.float32)[:, None] * inv_freq[None, :]


def reference(tokens, w_query, w_keyval, w_out, cache_keys, cache_values, lengths, positions):
    query = jnp.dot(tokens, w_query, preferred_element_type=jnp.float32).astype(jnp.bfloat16)
    keyval = jnp.dot(tokens, w_keyval, preferred_element_type=jnp.float32).astype(jnp.bfloat16)
    angles = rotary_angles(positions, HEAD_DIM)
    rot_query = rotate(query.astype(jnp.float32).reshape(ROWS, HEADS, HEAD_DIM), angles[:, None, :])
    rot_key = rotate(keyval[:, :HEAD_DIM].astype(jnp.float32), angles)
    new_value = keyval[:, HEAD_DIM:].astype(jnp.float32)
    score_scale = HEAD_DIM ** -0.5

    def one_row(items):
        row_query, row_keys, row_values, row_length, row_key, row_value = items
        scores = jnp.einsum("hd,td->ht", row_query, row_keys.astype(jnp.float32), precision=lax.Precision.HIGHEST) * score_scale
        visible = jnp.arange(CACHE, dtype=jnp.int32) < row_length
        scores = jnp.where(visible[None, :], scores, jnp.float32(-1e30))
        new_score = jnp.dot(row_query, row_key, precision=lax.Precision.HIGHEST) * score_scale
        highest = jnp.maximum(jnp.max(scores, axis=1), new_score)
        weights = jnp.where(visible[None, :], jnp.exp(scores - highest[:, None]), jnp.float32(0.0))
        new_weight = jnp.exp(new_score - highest)
        normaliser = jnp.sum(weights, axis=1) + new_weight
        summed = jnp.einsum("ht,td->hd", weights, row_values.astype(jnp.float32), precision=lax.Precision.HIGHEST)
        summed = summed + new_weight[:, None] * row_value[None, :]
        return summed / normaliser[:, None]

    out_heads = lax.map(one_row, (rot_query, cache_keys, cache_values, lengths, rot_key, new_value))
    out_heads = out_heads.reshape(ROWS, HQ).astype(jnp.bfloat16)
    return jnp.dot(out_heads, w_out, preferred_element_type=jnp.float32).astype(jnp.bfloat16)
```

```python
import functools
import math

import jax
import jax.numpy as jnp
from jax import lax
from jax.experimental import pallas as pl
from jax.experimental.pallas import tpu as pltpu
from jax.sharding import PartitionSpec as P

HEAD_DIM = 256
MESH = pl.DeviceIdType.MESH
VMEM_LIMIT = 64 * 1024 * 1024 - 65536


def merged(array, axis, combine):
    everything = jax.tree.map(lambda part: lax.all_gather(part, axis), array)
    leading = jax.tree.map(lambda part: part[0], everything)

    def hop(k, so_far):
        return combine(so_far, jax.tree.map(lambda part: part[k], everything))

    return lax.fori_loop(1, lax.axis_size(axis), hop, leading)


def rotate(vectors, angles):
    half_dim = vectors.shape[-1] // 2
    first_half = vectors[..., :half_dim]
    second_half = vectors[..., half_dim:]
    cosines = jnp.cos(angles)
    sines = jnp.sin(angles)
    return jnp.concatenate(
        [first_half * cosines - second_half * sines, first_half * sines + second_half * cosines],
        axis=-1,
    )


def rotary_angles(positions, head_dim):
    half_dim = head_dim // 2
    inv_freq = jnp.exp(-jnp.arange(half_dim, dtype=jnp.float32) * (math.log(10000.0) / half_dim))
    return positions.astype(jnp.float32)[:, None] * inv_freq[None, :]


def combine(former, latter):
    peak_a, mass_a, summed_a = former
    peak_b, mass_b, summed_b = latter
    highest = jnp.maximum(peak_a, peak_b)
    factor_a = jnp.exp(peak_a - highest)
    factor_b = jnp.exp(peak_b - highest)
    return (
        highest,
        mass_a * factor_a + mass_b * factor_b,
        summed_a * factor_a[..., None] + summed_b * factor_b[..., None],
    )


def body(tokens, w_query, w_keyval, w_out, cache_keys, cache_values, lengths, positions):
    query_cols = w_query.shape[1]
    block_rows = lax.all_gather(tokens, "yz", axis=0, tiled=True)
    partial_proj = jnp.concatenate(
        [
            jnp.dot(block_rows, w_query, preferred_element_type=jnp.float32),
            jnp.dot(block_rows, w_keyval, preferred_element_type=jnp.float32),
        ],
        axis=1,
    )
    query_part = partial_proj[:, :query_cols]
    keyval_part = partial_proj[:, query_cols:]
    query_sum, keyval_sum = lax.psum((query_part, keyval_part), "gx")
    query_full = query_sum.astype(jnp.bfloat16)
    keyval_full = keyval_sum.astype(jnp.bfloat16)
    query_rows, keyval_rows = (
        lax.all_to_all(query_full, "yz", split_axis=0, concat_axis=1, tiled=True),
        lax.all_to_all(keyval_full, "yz", split_axis=0, concat_axis=1, tiled=True),
    )
    row_count = query_rows.shape[0]
    head_count = query_rows.shape[1] // HEAD_DIM
    angles = rotary_angles(positions, HEAD_DIM)
    rot_query = rotate(
        query_rows.astype(jnp.float32).reshape(row_count, head_count, HEAD_DIM), angles[:, None, :]
    )
    rot_key = rotate(keyval_rows[:, :HEAD_DIM].astype(jnp.float32), angles)
    new_value = keyval_rows[:, HEAD_DIM:].astype(jnp.float32)
    score_scale = HEAD_DIM ** (-0.5)
    local_span = cache_keys.shape[1]
    slots_at = lax.axis_index("gx") * local_span + jnp.arange(local_span, dtype=jnp.int32)
    visible = slots_at[None, :] < lengths[:, None]
    scores = (
        jnp.einsum(
            "rhd,rtd->rht",
            rot_query,
            cache_keys.astype(jnp.float32),
            precision=lax.Precision.HIGHEST,
        )
        * score_scale
    )
    scores = jnp.where(visible[:, None, :], scores, jnp.float32(-1e30))
    row_peak = jnp.max(scores, axis=2)
    weights = jnp.where(
        visible[:, None, :], jnp.exp(scores - row_peak[..., None]), jnp.float32(0.0)
    )
    row_mass = jnp.sum(weights, axis=2)
    weighted = jnp.einsum(
        "rht,rtd->rhd", weights, cache_values.astype(jnp.float32), precision=lax.Precision.HIGHEST
    )
    row_peak, row_mass, weighted = merged((row_peak, row_mass, weighted), "gx", combine)
    new_score = (
        jnp.einsum("rhd,rd->rh", rot_query, rot_key, precision=lax.Precision.HIGHEST) * score_scale
    )
    highest = jnp.maximum(row_peak, new_score)
    old_factor = jnp.exp(row_peak - highest)
    new_weight = jnp.exp(new_score - highest)
    normaliser = row_mass * old_factor + new_weight
    summed = weighted * old_factor[..., None] + new_weight[..., None] * new_value[:, None, :]
    out_heads = (
        (summed / normaliser[..., None])
        .reshape(row_count, head_count * HEAD_DIM)
        .astype(jnp.bfloat16)
    )
    heads_local = lax.all_to_all(out_heads, "yz", split_axis=1, concat_axis=0, tiled=True)
    block_rows = heads_local
    attended = lax.psum_scatter(
        jnp.dot(block_rows, w_out, preferred_element_type=jnp.float32),
        "yz",
        scatter_dimension=0,
        tiled=True,
    )
    return attended.astype(jnp.bfloat16)


def fits(mesh, w_query):
    z_count, y_count = mesh.shape["gx"], mesh.shape["yz"]
    heads_local = w_query.shape[1] // HEAD_DIM // y_count
    return heads_local % z_count == 0 and z_count > 1 and y_count > 1 and (w_query.shape[0] // z_count) % 512 == 0


def split3(x):
    first = x.astype(jnp.bfloat16)
    rest = x - first.astype(jnp.float32)
    second = rest.astype(jnp.bfloat16)
    third = (rest - second.astype(jnp.float32)).astype(jnp.bfloat16)
    return first, second, third


def fused_kernel(
    dims,
    len_ref, tok_ref, cos_ref, sin_ref, wq_ref, wkv_ref, wo_ref, ck_ref, cv_ref,
    out_ref,
    wq, wkv, wo, kc, vc, tok, part, rbuf, kvp, kvr, kvs, kvin, qs, qin, ra, rb, rk,
    s_buf, sn_buf, st, str_, mg, lg, oa, ob, oar, obr, hs, xin, pout, prc,
    wq_sem, misc_sem, wo_sem, tok_s, tok_r, rs_s, rs_r, kv_s, kv_r, kv2_s, kv2_r,
    qd_s, qd_r, st_s, st_r, oa_s, oa_r, ob_s, ob_r, hd_s, hd_r, po_s, po_r,
):
    NZ, NY, R, HL, SLOTS, CH, NCH = dims
    HEADS = HL * NY
    HZ = HL // NZ
    W = HZ * HEAD_DIM
    z = lax.axis_index("gx")
    y = lax.axis_index("yz")
    f32 = jnp.float32

    def peer(dz, dy):
        return {"gx": lax.rem(z + dz, NZ), "yz": lax.rem(y + dy, NY)}

    def remote(src, dst, s, r, dev):
        return pltpu.make_async_remote_copy(
            src_ref=src, dst_ref=dst, send_sem=s, recv_sem=r, device_id=dev, device_id_type=MESH
        )

    SLOTSQ = wq.shape[0]

    def wq_copy(n):
        owner = lax.rem(z + n // HZ + 1, NZ)
        col = pl.multiple_of((owner * HZ + n % HZ) * HEAD_DIM, HEAD_DIM)
        slot = lax.rem(n, SLOTSQ)
        return pltpu.make_async_copy(wq_ref.at[:, pl.ds(col, HEAD_DIM)], wq.at[slot], wq_sem.at[slot])

    own_rows = pl.ds(pl.multiple_of(y * R, R), R)
    tok_local = pltpu.make_async_copy(tok_ref, tok.at[own_rows, :], misc_sem.at[0])
    tok_local.start()
    wkv_local = pltpu.make_async_copy(wkv_ref, wkv, misc_sem.at[1])
    kc_local = pltpu.make_async_copy(ck_ref, kc, misc_sem.at[2])
    vc_local = pltpu.make_async_copy(cv_ref, vc.at[:, pl.ds(0, SLOTS), :], misc_sem.at[3])

    barrier = pltpu.get_barrier_semaphore()

    @pl.loop(1, NZ * NY)
    def _(o):
        pl.semaphore_signal(barrier, inc=1, device_id=peer(o // NY, o % NY), device_id_type=MESH)

    pl.semaphore_wait(barrier, NZ * NY - 1)

    def tok_copy(d):
        return remote(tok_ref, tok.at[own_rows, :], tok_s.at[d - 1], tok_r.at[d - 1], peer(0, d))

    for d in range(1, NY):
        tok_copy(d).start()
    wkv_local.start()

    @pl.loop(0, SLOTSQ)
    def _(n):
        wq_copy(n).start()

    kc_local.start()
    vc_local.start()

    def wo_copy(n):
        col = pl.multiple_of(n * CH, CH)
        return pltpu.make_async_copy(wo_ref.at[:, pl.ds(col, CH)], wo.at[n], wo_sem.at[n])

    tok_local.wait()
    for d in range(1, NY):
        tok_copy(d).wait_recv()

    wkv_local.wait()
    kvp[...] = jnp.dot(tok[...], wkv[...], preferred_element_type=f32)

    def kv_copy(slot):
        return remote(kvp, kvr.at[slot], kv_s, kv_r.at[slot], {"gx": 0, "yz": y})

    for src in range(1, NZ):
        @pl.when(z == src)
        def _():
            kv_copy(src - 1).start()

    def rs_copy(n):
        return remote(part.at[n], rbuf.at[n], rs_s.at[n], rs_r.at[n], peer(n // HZ + 1, 0))

    def project(n):
        wq_copy(n).wait()
        part[n] = jnp.dot(tok[...], wq[lax.rem(n, SLOTSQ)], preferred_element_type=f32)

        @pl.when(n + SLOTSQ < HL)
        def _():
            wq_copy(n + SLOTSQ).start()

    REM = HL - HZ

    @pl.loop(0, REM)
    def _(n):
        project(n)
        rs_copy(n).start()

    @pl.loop(REM, HL)
    def _(n):
        project(n)

    @pl.loop(0, NCH)
    def _(n):
        wo_copy(n).start()

    def kv2_copy(d):
        target = lax.rem(y + d, NY)
        rows = pl.ds(pl.multiple_of(target * R, R), R)
        return remote(kvs.at[rows, :], kvin.at[y], kv2_s.at[d - 1], kv2_r.at[d - 1], {"gx": 0, "yz": target})

    @pl.when(z == 0)
    def _():
        total = kvp[...]
        for src in range(1, NZ):
            kv_copy(src - 1).wait_recv()
            total = total + kvr[src - 1]
        kvs[...] = total.astype(jnp.bfloat16)
        for d in range(1, NY):
            kv2_copy(d).start()
        kvin[y] = kvs[own_rows, :]

    @pl.when(z != 0)
    def _():
        kvin[...] = jnp.zeros_like(kvin)

    for i in range(HZ):
        total = part[REM + i]
        for d in range(1, NZ):
            n = (d - 1) * HZ + i
            rs_copy(n).wait_recv()
            total = total + rbuf[n]
        qs[:, i * HEAD_DIM:(i + 1) * HEAD_DIM] = total.astype(jnp.bfloat16)

    own_cols = pl.ds(pl.multiple_of((y * NZ + z) * W, W), W)

    def qd_copy(o):
        target = lax.rem(y + o % NY, NY)
        rows = pl.ds(pl.multiple_of(target * R, R), R)
        return remote(qs.at[rows, :], qin.at[:, own_cols], qd_s.at[o - 1], qd_r.at[o - 1], peer(o // NY, o % NY))

    @pl.loop(1, NZ * NY)
    def _(o):
        qd_copy(o).start()

    qin[:, own_cols] = qs[own_rows, :]
    kc_local.wait()
    vc_local.wait()

    cosines = cos_ref[...]
    sines = sin_ref[...]
    half = HEAD_DIM // 2

    @pl.when(z == 0)
    def _():
        for d in range(1, NY):
            kv2_copy(d).wait_recv()

    quarter = kvin.shape[2]
    kv_all = jnp.concatenate([kvin[k].astype(f32) for k in range(NY)], axis=1)
    ka = kv_all[:, :half]
    kb = kv_all[:, half:HEAD_DIM]
    rk[:, :half] = ka * cosines - kb * sines
    rk[:, half:HEAD_DIM] = ka * sines + kb * cosines
    rk[:, HEAD_DIM:] = kv_all[:, HEAD_DIM:]
    st[...] = jnp.zeros_like(st)

    @pl.loop(1, NZ * NY)
    def _(o):
        qd_copy(o).wait_recv()

    @pl.loop(0, HEADS)
    def _(p):
        owner = p // HL
        head = (p % HL) // HZ * HL + owner * HZ + p % HZ
        cols = pl.ds(pl.multiple_of(head * HEAD_DIM, HEAD_DIM), HEAD_DIM)
        x = qin[:, cols].astype(f32)
        a = x[:, :half]
        b = x[:, half:]
        rows = pl.ds(pl.multiple_of(p * R, R), R)
        ra[rows, :] = a * cosines - b * sines
        rb[rows, :] = a * sines + b * cosines

    scale = HEAD_DIM ** (-0.5)
    over_last = (((1,), (1,)), ((), ()))
    over_first = (((0,), (0,)), ((), ()))
    first_z = z == 0

    @pl.loop(0, R)
    def _(r):
        picked = pl.ds(r, HEADS, stride=R)
        q = jnp.concatenate([ra[picked, :], rb[picked, :]], axis=1)
        keys = kc[r]
        s = sum(lax.dot_general(keys, piece, over_last, preferred_element_type=f32) for piece in split3(q)) * scale
        slot = z * SLOTS + lax.broadcasted_iota(jnp.int32, (SLOTS, HEADS), 0)
        visible = slot < len_ref[r]
        s = jnp.where(visible, s, f32(-1e30))
        key_row = jnp.broadcast_to(rk[pl.ds(r, 1), :HEAD_DIM], (8, HEAD_DIM))
        s_new = lax.dot_general(
            key_row, q, over_last, precision=lax.Precision.HIGHEST, preferred_element_type=f32
        )[0:1, :] * scale
        s_new = jnp.where(first_z, s_new, f32(-1e30))
        peak = jnp.maximum(jnp.max(s, axis=0, keepdims=True), s_new)
        mass = jnp.sum(jnp.where(visible, jnp.exp(s - peak), f32(0.0)), axis=0, keepdims=True)
        mass = mass + jnp.where(first_z, jnp.exp(s_new - peak), f32(0.0))
        s_buf[r] = s
        sn_buf[pl.ds(r, 1), :] = s_new
        st[0, pl.ds(r, 1), 0:HEADS] = peak
        st[1, pl.ds(r, 1), 0:HEADS] = mass
        row = lax.broadcasted_iota(jnp.int32, (16, HEAD_DIM), 0)
        value = jnp.broadcast_to(rk[pl.ds(r, 1), HEAD_DIM:], (16, HEAD_DIM))
        vc[r, SLOTS:SLOTS + 16, :] = jnp.where(row == 0, value, f32(0.0)).astype(jnp.bfloat16)

    def st_copy(d):
        return remote(st, str_.at[d - 1], st_s.at[d - 1], st_r.at[d - 1], peer(d, 0))

    for d in range(1, NZ):
        st_copy(d).start()
    for d in range(1, NZ):
        st_copy(d).wait_recv()
    peak = st[0]
    for d in range(1, NZ):
        peak = jnp.maximum(peak, str_[d - 1, 0])
    mass = st[1] * jnp.exp(st[0] - peak)
    for d in range(1, NZ):
        mass = mass + str_[d - 1, 1] * jnp.exp(str_[d - 1, 0] - peak)
    mg[...] = peak
    lg[...] = mass

    @pl.loop(0, R)
    def _(r):
        peak = mg[pl.ds(r, 1), 0:HEADS]
        mass = lg[pl.ds(r, 1), 0:HEADS]
        p = jnp.exp(s_buf[r] - peak) / mass
        p_new = jnp.exp(sn_buf[pl.ds(r, 1), :] - peak) / mass
        row = lax.broadcasted_iota(jnp.int32, (16, HEADS), 0)
        p_new = jnp.where(row == 0, jnp.broadcast_to(p_new, (16, HEADS)), f32(0.0))
        p_all = jnp.concatenate([p, p_new], axis=0)
        values = vc[r]
        acc = sum(lax.dot_general(piece, values, over_first, preferred_element_type=f32) for piece in split3(p_all))
        picked = pl.ds(r, HEADS, stride=R)
        oa[picked, :] = acc[:, :half]
        ob[picked, :] = acc[:, half:]

    def o_copies(d):
        target = lax.rem(z + d, NZ)
        rows = pl.ds(pl.multiple_of(target * HL * R, HL * R), HL * R)
        return (
            remote(oa.at[rows, :], oar.at[d - 1], oa_s.at[d - 1], oa_r.at[d - 1], peer(d, 0)),
            remote(ob.at[rows, :], obr.at[d - 1], ob_s.at[d - 1], ob_r.at[d - 1], peer(d, 0)),
        )

    for d in range(1, NZ):
        for copy in o_copies(d):
            copy.start()
    for d in range(1, NZ):
        for copy in o_copies(d):
            copy.wait_recv()
    for k in range(HL):
        rows = pl.ds(pl.multiple_of(z * HL * R + k * R, R), R)
        ta = oa[rows, :]
        tb = ob[rows, :]
        for d in range(1, NZ):
            ta = ta + oar[d - 1, k * R:(k + 1) * R, :]
            tb = tb + obr[d - 1, k * R:(k + 1) * R, :]
        block, i = k // HZ, k % HZ
        hs[block * R:(block + 1) * R, i * HEAD_DIM:i * HEAD_DIM + half] = ta.astype(jnp.bfloat16)
        hs[block * R:(block + 1) * R, i * HEAD_DIM + half:(i + 1) * HEAD_DIM] = tb.astype(jnp.bfloat16)

    z_cols = pl.ds(pl.multiple_of(z * W, W), W)

    def hd_copy(o):
        target = lax.rem(y + o % NY, NY)
        rows = pl.ds(pl.multiple_of(target * R, R), R)
        return remote(hs.at[rows, :], xin.at[own_rows, z_cols], hd_s.at[o - 1], hd_r.at[o - 1], peer(o // NY, o % NY))

    @pl.loop(1, NZ * NY)
    def _(o):
        hd_copy(o).start()

    xin[own_rows, z_cols] = hs[own_rows, :]

    @pl.loop(1, NZ * NY)
    def _(o):
        hd_copy(o).wait_recv()

    def po_copy(n, d):
        target = lax.rem(y + d, NY)
        rows = pl.ds(pl.multiple_of(target * R, R), R)
        return remote(
            pout.at[n, rows, :], prc.at[d - 1, n], po_s.at[d - 1, n], po_r.at[d - 1, n], peer(0, d)
        )

    @pl.loop(0, NCH)
    def _(n):
        wo_copy(n).wait()
        pout[n] = jnp.dot(xin[...], wo[n], preferred_element_type=f32)
        for d in range(1, NY):
            po_copy(n, d).start()

    @pl.loop(0, NCH)
    def _(n):
        total = pout[n, own_rows, :]
        for d in range(1, NY):
            po_copy(n, d).wait_recv()
            total = total + prc[d - 1, n]
        out_ref[:, pl.ds(pl.multiple_of(n * CH, CH), CH)] = total.astype(jnp.bfloat16)

    for d in range(1, NY):
        tok_copy(d).wait_send()
    for src in range(1, NZ):
        @pl.when(z == src)
        def _():
            kv_copy(src - 1).wait_send()

    @pl.when(z == 0)
    def _():
        for d in range(1, NY):
            kv2_copy(d).wait_send()

    @pl.loop(0, REM)
    def _(n):
        rs_copy(n).wait_send()

    @pl.loop(1, NZ * NY)
    def _(o):
        qd_copy(o).wait_send()
        hd_copy(o).wait_send()

    for d in range(1, NZ):
        st_copy(d).wait_send()
        for copy in o_copies(d):
            copy.wait_send()

    @pl.loop(0, NCH)
    def _(n):
        for d in range(1, NY):
            po_copy(n, d).wait_send()


def fused_body(NZ, NY, tokens, w_query, w_keyval, w_out, cache_keys, cache_values, lengths, positions):
    R, DZ = tokens.shape
    HL = w_query.shape[1] // HEAD_DIM
    HZ = HL // NZ
    W = HZ * HEAD_DIM
    HEADS = HL * NY
    SLOTS = cache_keys.shape[1]
    DO = w_out.shape[1]
    CH = 512
    NCH = DO // CH
    half = HEAD_DIM // 2
    KV = w_keyval.shape[1]
    angles = rotary_angles(positions, HEAD_DIM)
    bf16, f32 = jnp.bfloat16, jnp.float32
    V = pltpu.VMEM
    D = pltpu.SemaphoreType.DMA
    slots_q = min(HL, 8)
    peers = NZ * NY - 1
    anyspec = pl.BlockSpec(memory_space=pl.ANY)
    vspec = pl.BlockSpec(memory_space=pltpu.VMEM)
    scratch = [
        V((slots_q, DZ, HEAD_DIM), bf16), V((DZ, KV), bf16), V((NCH, w_out.shape[0], CH), bf16),
        V((R, SLOTS, HEAD_DIM), bf16), V((R, SLOTS + 16, HEAD_DIM), bf16),
        V((R * NY, DZ), bf16), V((HL, R * NY, HEAD_DIM), f32), V((HL - HZ, R * NY, HEAD_DIM), f32),
        V((R * NY, KV), f32), V((NZ - 1, R * NY, KV), f32), V((R * NY, KV), bf16), V((NY, R, KV), bf16),
        V((R * NY, W), bf16), V((R, HEADS * HEAD_DIM), bf16),
        V((HEADS * R, half), f32), V((HEADS * R, half), f32), V((R, 2 * HEAD_DIM), f32),
        V((R, SLOTS, HEADS), f32), V((R, HEADS), f32),
        V((2, R, 128), f32), V((NZ - 1, 2, R, 128), f32), V((R, 128), f32), V((R, 128), f32),
        V((HEADS * R, half), f32), V((HEADS * R, half), f32),
        V((NZ - 1, HL * R, half), f32), V((NZ - 1, HL * R, half), f32),
        V((R * NY, W), bf16), V((R * NY, HL * HEAD_DIM), bf16),
        V((NCH, R * NY, CH), f32), V((NY - 1, NCH, R, CH), f32),
        D((slots_q,)), D((4,)), D((NCH,)), D((NY - 1,)), D((NY - 1,)),
        D((HL - HZ,)), D((HL - HZ,)), D, D((NZ - 1,)), D((NY - 1,)), D((NY - 1,)),
        D((peers,)), D((peers,)), D((NZ - 1,)), D((NZ - 1,)),
        D((NZ - 1,)), D((NZ - 1,)), D((NZ - 1,)), D((NZ - 1,)),
        D((peers,)), D((peers,)), D((NY - 1, NCH)), D((NY - 1, NCH)),
    ]
    return pl.pallas_call(
        functools.partial(fused_kernel, (NZ, NY, R, HL, SLOTS, CH, NCH)),
        out_shape=jax.ShapeDtypeStruct((R, DO), bf16),
        in_specs=[pl.BlockSpec(memory_space=pltpu.SMEM), anyspec, vspec, vspec] + [anyspec] * 5,
        out_specs=vspec,
        scratch_shapes=scratch,
        compiler_params=pltpu.CompilerParams(
            collective_id=0, has_side_effects=True, vmem_limit_bytes=VMEM_LIMIT
        ),
    )(lengths, tokens, jnp.cos(angles), jnp.sin(angles), w_query, w_keyval, w_out, cache_keys, cache_values)


def solution(mesh):
    placed = (
        P(("ga", "yz"), "gx"),
        P("gx", "yz"),
        P("gx", "yz"),
        P("yz", "gx"),
        P(("ga", "yz"), "gx", None),
        P(("ga", "yz"), "gx", None),
        P(("ga", "yz")),
        P(("ga", "yz")),
    )

    def run(*arrays):
        chosen = body
        if fits(mesh, arrays[1]):
            chosen = functools.partial(fused_body, mesh.shape["gx"], mesh.shape["yz"])
        return jax.shard_map(
            chosen, mesh=mesh, in_specs=placed, out_specs=P(("ga", "yz"), "gx"), check_vma=False
        )(*arrays)

    return run
```

```python
import functools
import math

import jax
import jax.numpy as jnp
from jax import lax
from jax.experimental import pallas as pl
from jax.experimental.pallas import tpu as pltpu
from jax.sharding import PartitionSpec as P

HEAD_DIM = 256
MESH = pl.DeviceIdType.MESH
VMEM_LIMIT = 64 * 1024 * 1024 - 65536


def merged(array, axis, combine):
    everything = jax.tree.map(lambda part: lax.all_gather(part, axis), array)
    leading = jax.tree.map(lambda part: part[0], everything)

    def hop(k, so_far):
        return combine(so_far, jax.tree.map(lambda part: part[k], everything))

    return lax.fori_loop(1, lax.axis_size(axis), hop, leading)


def rotate(vectors, angles):
    half_dim = vectors.shape[-1] // 2
    first_half = vectors[..., :half_dim]
    second_half = vectors[..., half_dim:]
    cosines = jnp.cos(angles)
    sines = jnp.sin(angles)
    return jnp.concatenate(
        [first_half * cosines - second_half * sines, first_half * sines + second_half * cosines],
        axis=-1,
    )


def rotary_angles(positions, head_dim):
    half_dim = head_dim // 2
    inv_freq = jnp.exp(-jnp.arange(half_dim, dtype=jnp.float32) * (math.log(10000.0) / half_dim))
    return positions.astype(jnp.float32)[:, None] * inv_freq[None, :]


def combine(former, latter):
    peak_a, mass_a, summed_a = former
    peak_b, mass_b, summed_b = latter
    highest = jnp.maximum(peak_a, peak_b)
    factor_a = jnp.exp(peak_a - highest)
    factor_b = jnp.exp(peak_b - highest)
    return (
        highest,
        mass_a * factor_a + mass_b * factor_b,
        summed_a * factor_a[..., None] + summed_b * factor_b[..., None],
    )


def body(tokens, w_query, w_keyval, w_out, cache_keys, cache_values, lengths, positions):
    query_cols = w_query.shape[1]
    block_rows = lax.all_gather(tokens, "yz", axis=0, tiled=True)
    partial_proj = jnp.concatenate(
        [
            jnp.dot(block_rows, w_query, preferred_element_type=jnp.float32),
            jnp.dot(block_rows, w_keyval, preferred_element_type=jnp.float32),
        ],
        axis=1,
    )
    query_part = partial_proj[:, :query_cols]
    keyval_part = partial_proj[:, query_cols:]
    query_sum, keyval_sum = lax.psum((query_part, keyval_part), "gx")
    query_full = query_sum.astype(jnp.bfloat16)
    keyval_full = keyval_sum.astype(jnp.bfloat16)
    query_rows, keyval_rows = (
        lax.all_to_all(query_full, "yz", split_axis=0, concat_axis=1, tiled=True),
        lax.all_to_all(keyval_full, "yz", split_axis=0, concat_axis=1, tiled=True),
    )
    row_count = query_rows.shape[0]
    head_count = query_rows.shape[1] // HEAD_DIM
    angles = rotary_angles(positions, HEAD_DIM)
    rot_query = rotate(
        query_rows.astype(jnp.float32).reshape(row_count, head_count, HEAD_DIM), angles[:, None, :]
    )
    rot_key = rotate(keyval_rows[:, :HEAD_DIM].astype(jnp.float32), angles)
    new_value = keyval_rows[:, HEAD_DIM:].astype(jnp.float32)
    score_scale = HEAD_DIM ** (-0.5)
    local_span = cache_keys.shape[1]
    slots_at = lax.axis_index("gx") * local_span + jnp.arange(local_span, dtype=jnp.int32)
    visible = slots_at[None, :] < lengths[:, None]
    scores = (
        jnp.einsum(
            "rhd,rtd->rht",
            rot_query,
            cache_keys.astype(jnp.float32),
            precision=lax.Precision.HIGHEST,
        )
        * score_scale
    )
    scores = jnp.where(visible[:, None, :], scores, jnp.float32(-1e30))
    row_peak = jnp.max(scores, axis=2)
    weights = jnp.where(
        visible[:, None, :], jnp.exp(scores - row_peak[..., None]), jnp.float32(0.0)
    )
    row_mass = jnp.sum(weights, axis=2)
    weighted = jnp.einsum(
        "rht,rtd->rhd", weights, cache_values.astype(jnp.float32), precision=lax.Precision.HIGHEST
    )
    row_peak, row_mass, weighted = merged((row_peak, row_mass, weighted), "gx", combine)
    new_score = (
        jnp.einsum("rhd,rd->rh", rot_query, rot_key, precision=lax.Precision.HIGHEST) * score_scale
    )
    highest = jnp.maximum(row_peak, new_score)
    old_factor = jnp.exp(row_peak - highest)
    new_weight = jnp.exp(new_score - highest)
    normaliser = row_mass * old_factor + new_weight
    summed = weighted * old_factor[..., None] + new_weight[..., None] * new_value[:, None, :]
    out_heads = (
        (summed / normaliser[..., None])
        .reshape(row_count, head_count * HEAD_DIM)
        .astype(jnp.bfloat16)
    )
    heads_local = lax.all_to_all(out_heads, "yz", split_axis=1, concat_axis=0, tiled=True)
    block_rows = heads_local
    attended = lax.psum_scatter(
        jnp.dot(block_rows, w_out, preferred_element_type=jnp.float32),
        "yz",
        scatter_dimension=0,
        tiled=True,
    )
    return attended.astype(jnp.bfloat16)


def fits(mesh, w_query):
    z_count, y_count = mesh.shape["gx"], mesh.shape["yz"]
    heads_local = w_query.shape[1] // HEAD_DIM // y_count
    return z_count == 4 and y_count == 4 and heads_local % 4 == 0


def split3(x):
    first = x.astype(jnp.bfloat16)
    rest = x - first.astype(jnp.float32)
    second = rest.astype(jnp.bfloat16)
    third = (rest - second.astype(jnp.float32)).astype(jnp.bfloat16)
    return first, second, third


def fused_kernel(
    dims,
    len_ref, tok_ref, cos_ref, sin_ref, wq_ref, wkv_ref, wo_ref, ck_ref, cv_ref,
    out_ref,
    wq, wkv, wo, kc, vc, tok, part, rbuf, kvp, kvr, kvs, kvin, qs, qin, ra, rb, rk,
    s_buf, sn_buf, st, str_, mg, lg, oa, ob, oar, obr, hs, xin, pout, prc,
    wq_sem, misc_sem, wo_sem, tok_s, tok_r, rs_s, rs_r, kv_s, kv_r, kv2_s, kv2_r,
    qd_s, qd_r, st_s, st_r, oa_s, oa_r, ob_s, ob_r, hd_s, hd_r, po_s, po_r,
):
    NZ, NY, R, HL, SLOTS, CH, NCH = dims
    HEADS = HL * NY
    HZ = HL // NZ
    W = HZ * HEAD_DIM
    z = lax.axis_index("gx")
    y = lax.axis_index("yz")
    f32 = jnp.float32

    def peer(dz, dy):
        return {"gx": lax.rem(z + dz, NZ), "yz": lax.rem(y + dy, NY)}

    def remote(src, dst, s, r, dev):
        return pltpu.make_async_remote_copy(
            src_ref=src, dst_ref=dst, send_sem=s, recv_sem=r, device_id=dev, device_id_type=MESH
        )

    SLOTSQ = wq.shape[0]

    def wq_copy(n):
        owner = z ^ (NZ - 1 - n // HZ)
        col = pl.multiple_of((owner * HZ + n % HZ) * HEAD_DIM, HEAD_DIM)
        slot = lax.rem(n, SLOTSQ)
        return pltpu.make_async_copy(wq_ref.at[:, pl.ds(col, HEAD_DIM)], wq.at[slot], wq_sem.at[slot])

    own_rows = pl.ds(pl.multiple_of(y * R, R), R)
    tok_local = pltpu.make_async_copy(tok_ref, tok.at[own_rows, :], misc_sem.at[0])
    tok_local.start()
    wkv_local = pltpu.make_async_copy(wkv_ref, wkv, misc_sem.at[1])
    kc_local = pltpu.make_async_copy(ck_ref, kc, misc_sem.at[2])
    vc_local = pltpu.make_async_copy(cv_ref, vc.at[:, pl.ds(0, SLOTS), :], misc_sem.at[3])

    barrier = pltpu.get_barrier_semaphore()

    @pl.loop(1, NZ * NY)
    def _(o):
        pl.semaphore_signal(barrier, inc=1, device_id=peer(o // NY, o % NY), device_id_type=MESH)

    pl.semaphore_wait(barrier, NZ * NY - 1)

    far_rows = pl.ds(pl.multiple_of((y ^ 2) * R, R), R)

    def tok_copy(k):
        src = tok.at[far_rows, :] if k == 2 else tok_ref
        rows = far_rows if k == 2 else own_rows
        return remote(src, tok.at[rows, :], tok_s.at[k], tok_r.at[k], {"gx": z, "yz": y ^ (2 if k == 1 else 1)})

    tok_copy(1).start()
    tok_copy(0).start()
    wkv_local.start()

    @pl.loop(0, SLOTSQ)
    def _(n):
        wq_copy(n).start()

    kc_local.start()
    vc_local.start()

    def wo_copy(n):
        col = pl.multiple_of(n * CH, CH)
        return pltpu.make_async_copy(wo_ref.at[:, pl.ds(col, CH)], wo.at[n], wo_sem.at[n])

    tok_copy(1).wait_recv()
    tok_copy(2).start()
    tok_local.wait()
    tok_copy(0).wait_recv()
    tok_copy(2).wait_recv()

    wkv_local.wait()
    kvp[...] = jnp.dot(tok[...], wkv[...], preferred_element_type=f32)

    def kv_copy(slot):
        return remote(kvp, kvr.at[slot], kv_s, kv_r.at[slot], {"gx": 0, "yz": y})

    for src in range(1, NZ):
        @pl.when(z == src)
        def _():
            kv_copy(src - 1).start()

    def rs_copy(n, step):
        return remote(part.at[n], rbuf.at[n], rs_s.at[n], rs_r.at[n], {"gx": z ^ (2 if step == 1 else 1), "yz": y})

    def project(n):
        wq_copy(n).wait()
        part[n] = jnp.dot(tok[...], wq[lax.rem(n, SLOTSQ)], preferred_element_type=f32)

        @pl.when(n + SLOTSQ < HL)
        def _():
            wq_copy(n + SLOTSQ).start()

    REM = HL - HZ

    @pl.loop(0, HZ)
    def _(n):
        project(n)
        rs_copy(n, 0).start()

    @pl.loop(HZ, 2 * HZ)
    def _(n):
        project(n)
        rs_copy(n - HZ, 0).wait_recv()
        part[n] = part[n] + rbuf[n - HZ]
        rs_copy(n, 1).start()

    @pl.loop(2 * HZ, REM)
    def _(n):
        project(n)
        rs_copy(n, 2).start()

    @pl.loop(REM, HL)
    def _(n):
        project(n)

    @pl.loop(0, NCH)
    def _(n):
        wo_copy(n).start()

    def kv2_copy(d):
        target = lax.rem(y + d, NY)
        rows = pl.ds(pl.multiple_of(target * R, R), R)
        return remote(kvs.at[rows, :], kvin.at[y], kv2_s.at[d - 1], kv2_r.at[d - 1], {"gx": 0, "yz": target})

    @pl.when(z == 0)
    def _():
        total = kvp[...]
        for src in range(1, NZ):
            kv_copy(src - 1).wait_recv()
            total = total + kvr[src - 1]
        kvs[...] = total.astype(jnp.bfloat16)
        for d in range(1, NY):
            kv2_copy(d).start()
        kvin[y] = kvs[own_rows, :]

    @pl.when(z != 0)
    def _():
        kvin[...] = jnp.zeros_like(kvin)

    for i in range(HZ):
        total = part[REM + i]
        for step in (2, 1):
            n = step * HZ + i
            rs_copy(n, step).wait_recv()
            total = total + rbuf[n]
        qs[:, i * HEAD_DIM:(i + 1) * HEAD_DIM] = total.astype(jnp.bfloat16)

    own_cols = pl.ds(pl.multiple_of((y * NZ + z) * W, W), W)

    def qd_copy(o):
        target = lax.rem(y + o % NY, NY)
        rows = pl.ds(pl.multiple_of(target * R, R), R)
        return remote(qs.at[rows, :], qin.at[:, own_cols], qd_s.at[o - 1], qd_r.at[o - 1], peer(o // NY, o % NY))

    @pl.loop(1, NZ * NY)
    def _(o):
        qd_copy(o).start()

    qin[:, own_cols] = qs[own_rows, :]
    kc_local.wait()
    vc_local.wait()

    cosines = cos_ref[...]
    sines = sin_ref[...]
    half = HEAD_DIM // 2

    @pl.when(z == 0)
    def _():
        for d in range(1, NY):
            kv2_copy(d).wait_recv()

    quarter = kvin.shape[2]
    kv_all = jnp.concatenate([kvin[k].astype(f32) for k in range(NY)], axis=1)
    ka = kv_all[:, :half]
    kb = kv_all[:, half:HEAD_DIM]
    rk[:, :half] = ka * cosines - kb * sines
    rk[:, half:HEAD_DIM] = ka * sines + kb * cosines
    rk[:, HEAD_DIM:] = kv_all[:, HEAD_DIM:]
    st[...] = jnp.zeros_like(st)

    @pl.loop(1, NZ * NY)
    def _(o):
        qd_copy(o).wait_recv()

    @pl.loop(0, HEADS)
    def _(p):
        owner = p // HL
        head = (p % HL) // HZ * HL + owner * HZ + p % HZ
        cols = pl.ds(pl.multiple_of(head * HEAD_DIM, HEAD_DIM), HEAD_DIM)
        x = qin[:, cols].astype(f32)
        a = x[:, :half]
        b = x[:, half:]
        rows = pl.ds(pl.multiple_of(p * R, R), R)
        ra[rows, :] = a * cosines - b * sines
        rb[rows, :] = a * sines + b * cosines

    scale = HEAD_DIM ** (-0.5)
    over_last = (((1,), (1,)), ((), ()))
    over_first = (((0,), (0,)), ((), ()))
    first_z = z == 0

    @pl.loop(0, R)
    def _(r):
        picked = pl.ds(r, HEADS, stride=R)
        q = jnp.concatenate([ra[picked, :], rb[picked, :]], axis=1)
        keys = kc[r]
        s = sum(lax.dot_general(keys, piece, over_last, preferred_element_type=f32) for piece in split3(q)) * scale
        slot = z * SLOTS + lax.broadcasted_iota(jnp.int32, (SLOTS, HEADS), 0)
        visible = slot < len_ref[r]
        s = jnp.where(visible, s, f32(-1e30))
        key_row = jnp.broadcast_to(rk[pl.ds(r, 1), :HEAD_DIM], (8, HEAD_DIM))
        s_new = lax.dot_general(
            key_row, q, over_last, precision=lax.Precision.HIGHEST, preferred_element_type=f32
        )[0:1, :] * scale
        s_new = jnp.where(first_z, s_new, f32(-1e30))
        peak = jnp.maximum(jnp.max(s, axis=0, keepdims=True), s_new)
        mass = jnp.sum(jnp.where(visible, jnp.exp(s - peak), f32(0.0)), axis=0, keepdims=True)
        mass = mass + jnp.where(first_z, jnp.exp(s_new - peak), f32(0.0))
        s_buf[r] = s
        sn_buf[pl.ds(r, 1), :] = s_new
        st[0, pl.ds(r, 1), 0:HEADS] = peak
        st[1, pl.ds(r, 1), 0:HEADS] = mass
        row = lax.broadcasted_iota(jnp.int32, (16, HEAD_DIM), 0)
        value = jnp.broadcast_to(rk[pl.ds(r, 1), HEAD_DIM:], (16, HEAD_DIM))
        vc[r, SLOTS:SLOTS + 16, :] = jnp.where(row == 0, value, f32(0.0)).astype(jnp.bfloat16)

    def st_copy(d):
        return remote(st, str_.at[d - 1], st_s.at[d - 1], st_r.at[d - 1], peer(d, 0))

    for d in range(1, NZ):
        st_copy(d).start()
    for d in range(1, NZ):
        st_copy(d).wait_recv()
    peak = st[0]
    for d in range(1, NZ):
        peak = jnp.maximum(peak, str_[d - 1, 0])
    mass = st[1] * jnp.exp(st[0] - peak)
    for d in range(1, NZ):
        mass = mass + str_[d - 1, 1] * jnp.exp(str_[d - 1, 0] - peak)
    mg[...] = peak
    lg[...] = mass

    @pl.loop(0, R)
    def _(r):
        peak = mg[pl.ds(r, 1), 0:HEADS]
        mass = lg[pl.ds(r, 1), 0:HEADS]
        p = jnp.exp(s_buf[r] - peak) / mass
        p_new = jnp.exp(sn_buf[pl.ds(r, 1), :] - peak) / mass
        row = lax.broadcasted_iota(jnp.int32, (16, HEADS), 0)
        p_new = jnp.where(row == 0, jnp.broadcast_to(p_new, (16, HEADS)), f32(0.0))
        p_all = jnp.concatenate([p, p_new], axis=0)
        values = vc[r]
        acc = sum(lax.dot_general(piece, values, over_first, preferred_element_type=f32) for piece in split3(p_all))
        picked = pl.ds(r, HEADS, stride=R)
        oa[picked, :] = acc[:, :half]
        ob[picked, :] = acc[:, half:]

    def o_copies(d):
        target = lax.rem(z + d, NZ)
        rows = pl.ds(pl.multiple_of(target * HL * R, HL * R), HL * R)
        return (
            remote(oa.at[rows, :], oar.at[d - 1], oa_s.at[d - 1], oa_r.at[d - 1], peer(d, 0)),
            remote(ob.at[rows, :], obr.at[d - 1], ob_s.at[d - 1], ob_r.at[d - 1], peer(d, 0)),
        )

    for d in range(1, NZ):
        for copy in o_copies(d):
            copy.start()
    for d in range(1, NZ):
        for copy in o_copies(d):
            copy.wait_recv()
    for k in range(HL):
        rows = pl.ds(pl.multiple_of(z * HL * R + k * R, R), R)
        ta = oa[rows, :]
        tb = ob[rows, :]
        for d in range(1, NZ):
            ta = ta + oar[d - 1, k * R:(k + 1) * R, :]
            tb = tb + obr[d - 1, k * R:(k + 1) * R, :]
        block, i = k // HZ, k % HZ
        hs[block * R:(block + 1) * R, i * HEAD_DIM:i * HEAD_DIM + half] = ta.astype(jnp.bfloat16)
        hs[block * R:(block + 1) * R, i * HEAD_DIM + half:(i + 1) * HEAD_DIM] = tb.astype(jnp.bfloat16)

    z_cols = pl.ds(pl.multiple_of(z * W, W), W)

    def hd_copy(o):
        target = lax.rem(y + o % NY, NY)
        rows = pl.ds(pl.multiple_of(target * R, R), R)
        return remote(hs.at[rows, :], xin.at[own_rows, z_cols], hd_s.at[o - 1], hd_r.at[o - 1], peer(o // NY, o % NY))

    @pl.loop(1, NZ * NY)
    def _(o):
        hd_copy(o).start()

    xin[own_rows, z_cols] = hs[own_rows, :]

    def po_copy(n, k):
        target = y ^ (1, 3, 2)[k]
        rows = pl.ds(pl.multiple_of(target * R, R), R)
        return remote(
            pout.at[n, rows, :], prc.at[k, n], po_s.at[k, n], po_r.at[k, n], {"gx": z, "yz": y ^ (1, 1, 2)[k]}
        )

    def cross(n):
        po_copy(n, 1).wait_recv()
        pout[n, far_rows, :] = pout[n, far_rows, :] + prc[1, n]
        po_copy(n, 2).start()

    for dz in range(NZ):
        @pl.loop(max(1, dz * NY), (dz + 1) * NY)
        def _(o):
            hd_copy(o).wait_recv()

        depth = pl.ds(pl.multiple_of(lax.rem(z + NZ - dz, NZ) * W, W), W)
        block = xin[:, depth]

        @pl.loop(0, NCH)
        def _(n):
            if dz == 0:
                wo_copy(n).wait()
            product = jnp.dot(block, wo[n, depth, :], preferred_element_type=f32)
            pout[n] = product if dz == 0 else pout[n] + product
            if dz == NZ - 1:
                po_copy(n, 1).start()
                po_copy(n, 0).start()

                @pl.when(n > 0)
                def _():
                    cross(n - 1)

    cross(NCH - 1)

    @pl.loop(0, NCH)
    def _(n):
        total = pout[n, own_rows, :]
        for k in (0, 2):
            po_copy(n, k).wait_recv()
            total = total + prc[k, n]
        out_ref[:, pl.ds(pl.multiple_of(n * CH, CH), CH)] = total.astype(jnp.bfloat16)

    for k in range(3):
        tok_copy(k).wait_send()
    for src in range(1, NZ):
        @pl.when(z == src)
        def _():
            kv_copy(src - 1).wait_send()

    @pl.when(z == 0)
    def _():
        for d in range(1, NY):
            kv2_copy(d).wait_send()

    for step in range(3):
        @pl.loop(step * HZ, (step + 1) * HZ)
        def _(n):
            rs_copy(n, step).wait_send()

    @pl.loop(1, NZ * NY)
    def _(o):
        qd_copy(o).wait_send()
        hd_copy(o).wait_send()

    for d in range(1, NZ):
        st_copy(d).wait_send()
        for copy in o_copies(d):
            copy.wait_send()

    @pl.loop(0, NCH)
    def _(n):
        for k in range(3):
            po_copy(n, k).wait_send()


def fused_body(NZ, NY, tokens, w_query, w_keyval, w_out, cache_keys, cache_values, lengths, positions):
    R, DZ = tokens.shape
    HL = w_query.shape[1] // HEAD_DIM
    HZ = HL // NZ
    W = HZ * HEAD_DIM
    HEADS = HL * NY
    SLOTS = cache_keys.shape[1]
    DO = w_out.shape[1]
    CH = 512
    NCH = DO // CH
    half = HEAD_DIM // 2
    KV = w_keyval.shape[1]
    angles = rotary_angles(positions, HEAD_DIM)
    bf16, f32 = jnp.bfloat16, jnp.float32
    V = pltpu.VMEM
    D = pltpu.SemaphoreType.DMA
    slots_q = min(HL, 8)
    peers = NZ * NY - 1
    anyspec = pl.BlockSpec(memory_space=pl.ANY)
    vspec = pl.BlockSpec(memory_space=pltpu.VMEM)
    scratch = [
        V((slots_q, DZ, HEAD_DIM), bf16), V((DZ, KV), bf16), V((NCH, w_out.shape[0], CH), bf16),
        V((R, SLOTS, HEAD_DIM), bf16), V((R, SLOTS + 16, HEAD_DIM), bf16),
        V((R * NY, DZ), bf16), V((HL, R * NY, HEAD_DIM), f32), V((HL - HZ, R * NY, HEAD_DIM), f32),
        V((R * NY, KV), f32), V((NZ - 1, R * NY, KV), f32), V((R * NY, KV), bf16), V((NY, R, KV), bf16),
        V((R * NY, W), bf16), V((R, HEADS * HEAD_DIM), bf16),
        V((HEADS * R, half), f32), V((HEADS * R, half), f32), V((R, 2 * HEAD_DIM), f32),
        V((R, SLOTS, HEADS), f32), V((R, HEADS), f32),
        V((2, R, 128), f32), V((NZ - 1, 2, R, 128), f32), V((R, 128), f32), V((R, 128), f32),
        V((HEADS * R, half), f32), V((HEADS * R, half), f32),
        V((NZ - 1, HL * R, half), f32), V((NZ - 1, HL * R, half), f32),
        V((R * NY, W), bf16), V((R * NY, HL * HEAD_DIM), bf16),
        V((NCH, R * NY, CH), f32), V((NY - 1, NCH, R, CH), f32),
        D((slots_q,)), D((4,)), D((NCH,)), D((NY - 1,)), D((NY - 1,)),
        D((HL - HZ,)), D((HL - HZ,)), D, D((NZ - 1,)), D((NY - 1,)), D((NY - 1,)),
        D((peers,)), D((peers,)), D((NZ - 1,)), D((NZ - 1,)),
        D((NZ - 1,)), D((NZ - 1,)), D((NZ - 1,)), D((NZ - 1,)),
        D((peers,)), D((peers,)), D((NY - 1, NCH)), D((NY - 1, NCH)),
    ]
    return pl.pallas_call(
        functools.partial(fused_kernel, (NZ, NY, R, HL, SLOTS, CH, NCH)),
        out_shape=jax.ShapeDtypeStruct((R, DO), bf16),
        in_specs=[pl.BlockSpec(memory_space=pltpu.SMEM), anyspec, vspec, vspec] + [anyspec] * 5,
        out_specs=vspec,
        scratch_shapes=scratch,
        compiler_params=pltpu.CompilerParams(
            collective_id=0, has_side_effects=True, vmem_limit_bytes=VMEM_LIMIT
        ),
    )(lengths, tokens, jnp.cos(angles), jnp.sin(angles), w_query, w_keyval, w_out, cache_keys, cache_values)


def solution(mesh):
    placed = (
        P(("ga", "yz"), "gx"),
        P("gx", "yz"),
        P("gx", "yz"),
        P("yz", "gx"),
        P(("ga", "yz"), "gx", None),
        P(("ga", "yz"), "gx", None),
        P(("ga", "yz")),
        P(("ga", "yz")),
    )

    def run(*arrays):
        chosen = body
        if fits(mesh, arrays[1]):
            chosen = functools.partial(fused_body, mesh.shape["gx"], mesh.shape["yz"])
        return jax.shard_map(
            chosen, mesh=mesh, in_specs=placed, out_specs=P(("ga", "yz"), "gx"), check_vma=False
        )(*arrays)

    return run
```

```python
import functools
import math

import jax
import jax.numpy as jnp
from jax import lax
from jax.experimental import pallas as pl
from jax.experimental.pallas import tpu as pltpu
from jax.sharding import PartitionSpec as P

HEAD_DIM = 256
MESH = pl.DeviceIdType.MESH
VMEM_LIMIT = 64 * 1024 * 1024 - 65536


def merged(array, axis, combine):
    everything = jax.tree.map(lambda part: lax.all_gather(part, axis), array)
    leading = jax.tree.map(lambda part: part[0], everything)

    def hop(k, so_far):
        return combine(so_far, jax.tree.map(lambda part: part[k], everything))

    return lax.fori_loop(1, lax.axis_size(axis), hop, leading)


def rotate(vectors, angles):
    half_dim = vectors.shape[-1] // 2
    first_half = vectors[..., :half_dim]
    second_half = vectors[..., half_dim:]
    cosines = jnp.cos(angles)
    sines = jnp.sin(angles)
    return jnp.concatenate(
        [first_half * cosines - second_half * sines, first_half * sines + second_half * cosines],
        axis=-1,
    )


def rotary_angles(positions, head_dim):
    half_dim = head_dim // 2
    inv_freq = jnp.exp(-jnp.arange(half_dim, dtype=jnp.float32) * (math.log(10000.0) / half_dim))
    return positions.astype(jnp.float32)[:, None] * inv_freq[None, :]


def combine(former, latter):
    peak_a, mass_a, summed_a = former
    peak_b, mass_b, summed_b = latter
    highest = jnp.maximum(peak_a, peak_b)
    factor_a = jnp.exp(peak_a - highest)
    factor_b = jnp.exp(peak_b - highest)
    return (
        highest,
        mass_a * factor_a + mass_b * factor_b,
        summed_a * factor_a[..., None] + summed_b * factor_b[..., None],
    )


def body(tokens, w_query, w_keyval, w_out, cache_keys, cache_values, lengths, positions):
    query_cols = w_query.shape[1]
    block_rows = lax.all_gather(tokens, "yz", axis=0, tiled=True)
    partial_proj = jnp.concatenate(
        [
            jnp.dot(block_rows, w_query, preferred_element_type=jnp.float32),
            jnp.dot(block_rows, w_keyval, preferred_element_type=jnp.float32),
        ],
        axis=1,
    )
    query_part = partial_proj[:, :query_cols]
    keyval_part = partial_proj[:, query_cols:]
    query_sum, keyval_sum = lax.psum((query_part, keyval_part), "gx")
    query_full = query_sum.astype(jnp.bfloat16)
    keyval_full = keyval_sum.astype(jnp.bfloat16)
    query_rows, keyval_rows = (
        lax.all_to_all(query_full, "yz", split_axis=0, concat_axis=1, tiled=True),
        lax.all_to_all(keyval_full, "yz", split_axis=0, concat_axis=1, tiled=True),
    )
    row_count = query_rows.shape[0]
    head_count = query_rows.shape[1] // HEAD_DIM
    angles = rotary_angles(positions, HEAD_DIM)
    rot_query = rotate(
        query_rows.astype(jnp.float32).reshape(row_count, head_count, HEAD_DIM), angles[:, None, :]
    )
    rot_key = rotate(keyval_rows[:, :HEAD_DIM].astype(jnp.float32), angles)
    new_value = keyval_rows[:, HEAD_DIM:].astype(jnp.float32)
    score_scale = HEAD_DIM ** (-0.5)
    local_span = cache_keys.shape[1]
    slots_at = lax.axis_index("gx") * local_span + jnp.arange(local_span, dtype=jnp.int32)
    visible = slots_at[None, :] < lengths[:, None]
    scores = (
        jnp.einsum(
            "rhd,rtd->rht",
            rot_query,
            cache_keys.astype(jnp.float32),
            precision=lax.Precision.HIGHEST,
        )
        * score_scale
    )
    scores = jnp.where(visible[:, None, :], scores, jnp.float32(-1e30))
    row_peak = jnp.max(scores, axis=2)
    weights = jnp.where(
        visible[:, None, :], jnp.exp(scores - row_peak[..., None]), jnp.float32(0.0)
    )
    row_mass = jnp.sum(weights, axis=2)
    weighted = jnp.einsum(
        "rht,rtd->rhd", weights, cache_values.astype(jnp.float32), precision=lax.Precision.HIGHEST
    )
    row_peak, row_mass, weighted = merged((row_peak, row_mass, weighted), "gx", combine)
    new_score = (
        jnp.einsum("rhd,rd->rh", rot_query, rot_key, precision=lax.Precision.HIGHEST) * score_scale
    )
    highest = jnp.maximum(row_peak, new_score)
    old_factor = jnp.exp(row_peak - highest)
    new_weight = jnp.exp(new_score - highest)
    normaliser = row_mass * old_factor + new_weight
    summed = weighted * old_factor[..., None] + new_weight[..., None] * new_value[:, None, :]
    out_heads = (
        (summed / normaliser[..., None])
        .reshape(row_count, head_count * HEAD_DIM)
        .astype(jnp.bfloat16)
    )
    heads_local = lax.all_to_all(out_heads, "yz", split_axis=1, concat_axis=0, tiled=True)
    block_rows = heads_local
    attended = lax.psum_scatter(
        jnp.dot(block_rows, w_out, preferred_element_type=jnp.float32),
        "yz",
        scatter_dimension=0,
        tiled=True,
    )
    return attended.astype(jnp.bfloat16)


def fits(mesh, w_query):
    z_count, y_count = mesh.shape["gx"], mesh.shape["yz"]
    heads_local = w_query.shape[1] // HEAD_DIM // y_count
    return z_count == 4 and y_count == 4 and heads_local % 4 == 0


def split3(x):
    first = x.astype(jnp.bfloat16)
    rest = x - first.astype(jnp.float32)
    second = rest.astype(jnp.bfloat16)
    third = (rest - second.astype(jnp.float32)).astype(jnp.bfloat16)
    return first, second, third


def fused_kernel(
    dims,
    len_ref, tok_ref, cos_ref, sin_ref, wq_ref, wkv_ref, wo_ref, ck_ref, cv_ref,
    out_ref,
    wq, wkv, wo, kc, vc, tok, part, rbuf, kvp, kvr, kvs, kvin, qs, qin, ra, rb, rk,
    st, str_, oa, ob, oar, obr, hs, xin, pout, prc,
    wq_sem, misc_sem, wo_sem, tok_s, tok_r, rs_s, rs_r, kv_s, kv_r, kv2_s, kv2_r,
    qd_s, qd_r, st_s, st_r, oa_s, oa_r, ob_s, ob_r, hd_s, hd_r, po_s, po_r,
):
    NZ, NY, R, HL, SLOTS, CH, NCH = dims
    HEADS = HL * NY
    HZ = HL // NZ
    W = HZ * HEAD_DIM
    z = lax.axis_index("gx")
    y = lax.axis_index("yz")
    f32 = jnp.float32

    def peer(dz, dy):
        return {"gx": lax.rem(z + dz, NZ), "yz": lax.rem(y + dy, NY)}

    def remote(src, dst, s, r, dev):
        return pltpu.make_async_remote_copy(
            src_ref=src, dst_ref=dst, send_sem=s, recv_sem=r, device_id=dev, device_id_type=MESH
        )

    SLOTSQ = wq.shape[0]

    def wq_copy(n):
        owner = lax.rem(z + n // HZ + 1, NZ)
        col = pl.multiple_of((owner * HZ + n % HZ) * HEAD_DIM, HEAD_DIM)
        slot = lax.rem(n, SLOTSQ)
        return pltpu.make_async_copy(wq_ref.at[:, pl.ds(col, HEAD_DIM)], wq.at[slot], wq_sem.at[slot])

    own_rows = pl.ds(pl.multiple_of(y * R, R), R)
    tok_local = pltpu.make_async_copy(tok_ref, tok.at[own_rows, :], misc_sem.at[0])
    tok_local.start()
    wkv_local = pltpu.make_async_copy(wkv_ref, wkv, misc_sem.at[1])
    kc_local = pltpu.make_async_copy(ck_ref, kc, misc_sem.at[2])
    vc_local = pltpu.make_async_copy(cv_ref, vc, misc_sem.at[3])

    barrier = pltpu.get_barrier_semaphore()

    @pl.loop(1, NZ * NY)
    def _(o):
        pl.semaphore_signal(barrier, inc=1, device_id=peer(o // NY, o % NY), device_id_type=MESH)

    pl.semaphore_wait(barrier, NZ * NY - 1)

    far_rows = pl.ds(pl.multiple_of((y ^ 2) * R, R), R)

    def tok_copy(d):
        return remote(tok_ref, tok.at[own_rows, :], tok_s.at[d - 1], tok_r.at[d - 1], peer(0, d))

    for d in range(1, NY):
        tok_copy(d).start()
    wkv_local.start()

    @pl.loop(0, SLOTSQ)
    def _(n):
        wq_copy(n).start()

    kc_local.start()
    vc_local.start()

    def wo_copy(n):
        col = pl.multiple_of(n * CH, CH)
        return pltpu.make_async_copy(wo_ref.at[:, pl.ds(col, CH)], wo.at[n], wo_sem.at[n])

    tok_local.wait()
    for d in range(1, NY):
        tok_copy(d).wait_recv()

    wkv_local.wait()
    kvp[...] = jnp.dot(tok[...], wkv[...], preferred_element_type=f32)

    def kv_copy(slot):
        return remote(kvp, kvr.at[slot], kv_s, kv_r.at[slot], {"gx": 0, "yz": y})

    for src in range(1, NZ):
        @pl.when(z == src)
        def _():
            kv_copy(src - 1).start()

    def rs_copy(n):
        return remote(part.at[n], rbuf.at[n], rs_s.at[n], rs_r.at[n], peer(n // HZ + 1, 0))

    def project(n):
        wq_copy(n).wait()
        part[n] = jnp.dot(tok[...], wq[lax.rem(n, SLOTSQ)], preferred_element_type=f32)

        @pl.when(n + SLOTSQ < HL)
        def _():
            wq_copy(n + SLOTSQ).start()

    REM = HL - HZ

    @pl.loop(0, REM)
    def _(n):
        project(n)
        rs_copy(n).start()

    @pl.loop(REM, HL)
    def _(n):
        project(n)

    @pl.loop(0, NCH)
    def _(n):
        wo_copy(n).start()

    def kv2_copy(d):
        target = lax.rem(y + d, NY)
        rows = pl.ds(pl.multiple_of(target * R, R), R)
        return remote(kvs.at[rows, :], kvin.at[y], kv2_s.at[d - 1], kv2_r.at[d - 1], {"gx": 0, "yz": target})

    @pl.when(z == 0)
    def _():
        total = kvp[...]
        for src in range(1, NZ):
            kv_copy(src - 1).wait_recv()
            total = total + kvr[src - 1]
        kvs[...] = total.astype(jnp.bfloat16)
        for d in range(1, NY):
            kv2_copy(d).start()
        kvin[y] = kvs[own_rows, :]

    @pl.when(z != 0)
    def _():
        kvin[...] = jnp.zeros_like(kvin)

    for i in range(HZ):
        total = part[REM + i]
        for d in range(1, NZ):
            n = (d - 1) * HZ + i
            rs_copy(n).wait_recv()
            total = total + rbuf[n]
        qs[:, i * HEAD_DIM:(i + 1) * HEAD_DIM] = total.astype(jnp.bfloat16)

    own_cols = pl.ds(pl.multiple_of((y * NZ + z) * W, W), W)

    def qd_copy(o):
        target = lax.rem(y + o % NY, NY)
        rows = pl.ds(pl.multiple_of(target * R, R), R)
        return remote(qs.at[rows, :], qin.at[:, own_cols], qd_s.at[o - 1], qd_r.at[o - 1], peer(o // NY, o % NY))

    @pl.loop(1, NZ * NY)
    def _(o):
        qd_copy(o).start()

    qin[:, own_cols] = qs[own_rows, :]
    kc_local.wait()
    vc_local.wait()

    cosines = cos_ref[...]
    sines = sin_ref[...]
    half = HEAD_DIM // 2

    @pl.when(z == 0)
    def _():
        for d in range(1, NY):
            kv2_copy(d).wait_recv()

    quarter = kvin.shape[2]
    kv_all = jnp.concatenate([kvin[k].astype(f32) for k in range(NY)], axis=1)
    ka = kv_all[:, :half]
    kb = kv_all[:, half:HEAD_DIM]
    rk[:, :half] = ka * cosines - kb * sines
    rk[:, half:HEAD_DIM] = ka * sines + kb * cosines
    rk[:, HEAD_DIM:] = kv_all[:, HEAD_DIM:]
    st[...] = jnp.zeros_like(st)

    @pl.loop(1, NZ * NY)
    def _(o):
        qd_copy(o).wait_recv()

    @pl.loop(0, HEADS)
    def _(p):
        owner = p // HL
        head = (p % HL) // HZ * HL + owner * HZ + p % HZ
        cols = pl.ds(pl.multiple_of(head * HEAD_DIM, HEAD_DIM), HEAD_DIM)
        x = qin[:, cols].astype(f32)
        a = x[:, :half]
        b = x[:, half:]
        rows = pl.ds(pl.multiple_of(p * R, R), R)
        ra[rows, :] = a * cosines - b * sines
        rb[rows, :] = a * sines + b * cosines

    scale = HEAD_DIM ** (-0.5)
    over_last = (((1,), (1,)), ((), ()))
    over_first = (((0,), (0,)), ((), ()))
    first_z = z == 0

    HALF = R // 2

    def o_copies(part_rows, d):
        target = lax.rem(z + d, NZ)
        size = HL * HALF
        rows = pl.ds(pl.multiple_of((part_rows * NZ + target) * size, size), size)
        return tuple(
            remote(src.at[rows, :], dst.at[d - 1, part_rows], snd.at[d - 1, part_rows], rcv.at[d - 1, part_rows], peer(d, 0))
            for src, dst, snd, rcv in ((oa, oar, oa_s, oa_r), (ob, obr, ob_s, ob_r))
        )

    def attend(r):
        picked = pl.ds(r, HEADS, stride=R)
        q = jnp.concatenate([ra[picked, :], rb[picked, :]], axis=1)
        keys = kc[r]
        s = sum(lax.dot_general(keys, piece, over_last, preferred_element_type=f32) for piece in split3(q)) * scale
        slot = z * SLOTS + lax.broadcasted_iota(jnp.int32, (SLOTS, HEADS), 0)
        visible = slot < len_ref[r]
        s = jnp.where(visible, s, f32(-1e30))
        key_row = jnp.broadcast_to(rk[pl.ds(r, 1), :HEAD_DIM], (8, HEAD_DIM))
        s_new = lax.dot_general(
            key_row, q, over_last, precision=lax.Precision.HIGHEST, preferred_element_type=f32
        )[0:1, :] * scale
        s_new = jnp.where(first_z, s_new, f32(-1e30))
        peak = jnp.maximum(jnp.max(s, axis=0, keepdims=True), s_new)
        p = jnp.where(visible, jnp.exp(s - peak), f32(0.0))
        p_new = jnp.where(first_z, jnp.exp(s_new - peak), f32(0.0))
        st[0, pl.ds(r, 1), 0:HEADS] = peak
        st[1, pl.ds(r, 1), 0:HEADS] = jnp.sum(p, axis=0, keepdims=True) + p_new
        row = lax.broadcasted_iota(jnp.int32, (16, HEAD_DIM), 0)
        value = jnp.broadcast_to(rk[pl.ds(r, 1), HEAD_DIM:], (16, HEAD_DIM))
        value = jnp.where(row == 0, value, f32(0.0)).astype(jnp.bfloat16)
        values = jnp.concatenate([vc[r, 0:SLOTS, :], value], axis=0)
        row = lax.broadcasted_iota(jnp.int32, (16, HEADS), 0)
        p_new = jnp.where(row == 0, jnp.broadcast_to(p_new, (16, HEADS)), f32(0.0))
        p_all = jnp.concatenate([p, p_new], axis=0)
        acc = sum(lax.dot_general(piece, values, over_first, preferred_element_type=f32) for piece in split3(p_all))
        placed = pl.ds(r // HALF * (HEADS * HALF) + r % HALF, HEADS, stride=HALF)
        oa[placed, :] = acc[:, :half]
        ob[placed, :] = acc[:, half:]

    for part_rows in range(2):
        pl.loop(part_rows * HALF, (part_rows + 1) * HALF)(attend)
        for d in range(1, NZ):
            for copy in o_copies(part_rows, d):
                copy.start()

    def st_copy(d):
        return remote(st, str_.at[d - 1], st_s.at[d - 1], st_r.at[d - 1], peer(d, 0))

    for d in range(1, NZ):
        st_copy(d).start()
    for d in range(1, NZ):
        st_copy(d).wait_recv()
    peaks = [st[0]] + [str_[d - 1, 0] for d in range(1, NZ)]
    masses = [st[1]] + [str_[d - 1, 1] for d in range(1, NZ)]
    highest = functools.reduce(jnp.maximum, peaks)
    factors = [jnp.exp(peak - highest) for peak in peaks]
    normaliser = sum(mass * factor for mass, factor in zip(masses, factors))
    factors = [factor / normaliser for factor in factors]
    lane = lax.broadcasted_iota(jnp.int32, (R, 128), 1)
    for part_rows in range(2):
        for d in range(1, NZ):
            for copy in o_copies(part_rows, d):
                copy.wait_recv()
    for k in range(HL):
        columns = [
            jnp.sum(jnp.where(lane == z * HL + k, factor, f32(0.0)), axis=1, keepdims=True) for factor in factors
        ]
        block, i = k // HZ, k % HZ
        for own, arrived, low in ((oa, oar, 0), (ob, obr, half)):
            pieces = []
            for h in range(2):
                mine = own[pl.ds(pl.multiple_of((h * NZ + z) * HL * HALF + k * HALF, HALF), HALF), :]
                total = mine * columns[0][h * HALF:(h + 1) * HALF]
                for d in range(1, NZ):
                    total = total + arrived[d - 1, h, k * HALF:(k + 1) * HALF, :] * columns[d][h * HALF:(h + 1) * HALF]
                pieces.append(total)
            both = jnp.concatenate(pieces, axis=0).astype(jnp.bfloat16)
            hs[block * R:(block + 1) * R, i * HEAD_DIM + low:i * HEAD_DIM + low + half] = both

    z_cols = pl.ds(pl.multiple_of(z * W, W), W)

    def hd_copy(o):
        target = lax.rem(y + o % NY, NY)
        rows = pl.ds(pl.multiple_of(target * R, R), R)
        return remote(hs.at[rows, :], xin.at[own_rows, z_cols], hd_s.at[o - 1], hd_r.at[o - 1], peer(o // NY, o % NY))

    @pl.loop(1, NZ * NY)
    def _(o):
        hd_copy(o).start()

    xin[own_rows, z_cols] = hs[own_rows, :]

    def po_copy(n, k):
        target = y ^ (1, 3, 2)[k]
        rows = pl.ds(pl.multiple_of(target * R, R), R)
        return remote(
            pout.at[n, rows, :], prc.at[k, n], po_s.at[k, n], po_r.at[k, n], {"gx": z, "yz": y ^ (1, 1, 2)[k]}
        )

    def cross(n):
        po_copy(n, 1).wait_recv()
        pout[n, far_rows, :] = pout[n, far_rows, :] + prc[1, n]
        po_copy(n, 2).start()

    for dz in range(NZ):
        @pl.loop(max(1, dz * NY), (dz + 1) * NY)
        def _(o):
            hd_copy(o).wait_recv()

        depth = pl.ds(pl.multiple_of(lax.rem(z + NZ - dz, NZ) * W, W), W)
        block = xin[:, depth]

        @pl.loop(0, NCH)
        def _(n):
            if dz == 0:
                wo_copy(n).wait()
            product = jnp.dot(block, wo[n, depth, :], preferred_element_type=f32)
            pout[n] = product if dz == 0 else pout[n] + product
            if dz == NZ - 1:
                po_copy(n, 1).start()
                po_copy(n, 0).start()

                @pl.when(n > 0)
                def _():
                    cross(n - 1)

    cross(NCH - 1)

    @pl.loop(0, NCH)
    def _(n):
        total = pout[n, own_rows, :]
        for k in (0, 2):
            po_copy(n, k).wait_recv()
            total = total + prc[k, n]
        out_ref[:, pl.ds(pl.multiple_of(n * CH, CH), CH)] = total.astype(jnp.bfloat16)

    for d in range(1, NY):
        tok_copy(d).wait_send()
    for src in range(1, NZ):
        @pl.when(z == src)
        def _():
            kv_copy(src - 1).wait_send()

    @pl.when(z == 0)
    def _():
        for d in range(1, NY):
            kv2_copy(d).wait_send()

    @pl.loop(0, REM)
    def _(n):
        rs_copy(n).wait_send()

    @pl.loop(1, NZ * NY)
    def _(o):
        qd_copy(o).wait_send()
        hd_copy(o).wait_send()

    for d in range(1, NZ):
        st_copy(d).wait_send()
        for part_rows in range(2):
            for copy in o_copies(part_rows, d):
                copy.wait_send()

    @pl.loop(0, NCH)
    def _(n):
        for k in range(3):
            po_copy(n, k).wait_send()


def fused_body(NZ, NY, tokens, w_query, w_keyval, w_out, cache_keys, cache_values, lengths, positions):
    R, DZ = tokens.shape
    HL = w_query.shape[1] // HEAD_DIM
    HZ = HL // NZ
    W = HZ * HEAD_DIM
    HEADS = HL * NY
    SLOTS = cache_keys.shape[1]
    DO = w_out.shape[1]
    CH = 512
    NCH = DO // CH
    half = HEAD_DIM // 2
    KV = w_keyval.shape[1]
    angles = rotary_angles(positions, HEAD_DIM)
    bf16, f32 = jnp.bfloat16, jnp.float32
    V = pltpu.VMEM
    D = pltpu.SemaphoreType.DMA
    slots_q = min(HL, 8)
    peers = NZ * NY - 1
    anyspec = pl.BlockSpec(memory_space=pl.ANY)
    vspec = pl.BlockSpec(memory_space=pltpu.VMEM)
    scratch = [
        V((slots_q, DZ, HEAD_DIM), bf16), V((DZ, KV), bf16), V((NCH, w_out.shape[0], CH), bf16),
        V((R, SLOTS, HEAD_DIM), bf16), V((R, SLOTS, HEAD_DIM), bf16),
        V((R * NY, DZ), bf16), V((HL, R * NY, HEAD_DIM), f32), V((HL - HZ, R * NY, HEAD_DIM), f32),
        V((R * NY, KV), f32), V((NZ - 1, R * NY, KV), f32), V((R * NY, KV), bf16), V((NY, R, KV), bf16),
        V((R * NY, W), bf16), V((R, HEADS * HEAD_DIM), bf16),
        V((HEADS * R, half), f32), V((HEADS * R, half), f32), V((R, 2 * HEAD_DIM), f32),
        V((2, R, 128), f32), V((NZ - 1, 2, R, 128), f32),
        V((HEADS * R, half), f32), V((HEADS * R, half), f32),
        V((NZ - 1, 2, HL * R // 2, half), f32), V((NZ - 1, 2, HL * R // 2, half), f32),
        V((R * NY, W), bf16), V((R * NY, HL * HEAD_DIM), bf16),
        V((NCH, R * NY, CH), f32), V((NY - 1, NCH, R, CH), f32),
        D((slots_q,)), D((4,)), D((NCH,)), D((NY - 1,)), D((NY - 1,)),
        D((HL - HZ,)), D((HL - HZ,)), D, D((NZ - 1,)), D((NY - 1,)), D((NY - 1,)),
        D((peers,)), D((peers,)), D((NZ - 1,)), D((NZ - 1,)),
        D((NZ - 1, 2)), D((NZ - 1, 2)), D((NZ - 1, 2)), D((NZ - 1, 2)),
        D((peers,)), D((peers,)), D((NY - 1, NCH)), D((NY - 1, NCH)),
    ]
    return pl.pallas_call(
        functools.partial(fused_kernel, (NZ, NY, R, HL, SLOTS, CH, NCH)),
        out_shape=jax.ShapeDtypeStruct((R, DO), bf16),
        in_specs=[pl.BlockSpec(memory_space=pltpu.SMEM), anyspec, vspec, vspec] + [anyspec] * 5,
        out_specs=vspec,
        scratch_shapes=scratch,
        compiler_params=pltpu.CompilerParams(
            collective_id=0, has_side_effects=True, vmem_limit_bytes=VMEM_LIMIT
        ),
    )(lengths, tokens, jnp.cos(angles), jnp.sin(angles), w_query, w_keyval, w_out, cache_keys, cache_values)


def solution(mesh):
    placed = (
        P(("ga", "yz"), "gx"),
        P("gx", "yz"),
        P("gx", "yz"),
        P("yz", "gx"),
        P(("ga", "yz"), "gx", None),
        P(("ga", "yz"), "gx", None),
        P(("ga", "yz")),
        P(("ga", "yz")),
    )

    def run(*arrays):
        chosen = body
        if fits(mesh, arrays[1]):
            chosen = functools.partial(fused_body, mesh.shape["gx"], mesh.shape["yz"])
        return jax.shard_map(
            chosen, mesh=mesh, in_specs=placed, out_specs=P(("ga", "yz"), "gx"), check_vma=False
        )(*arrays)

    return run
```
